128 devices in a mesh: attn: 8 (over z, x_lo), ffn: 16 (over y, x_hi, core).
Axes of the slice: x: 4 (x_hi: 2, x_lo: 2; x = x_hi * 2 + x_lo), y: 4, z: 4, core: 2. Of those that a mesh axis runs over, the one named last changes fastest.
Arguments:
- queries: bfloat16 [512, 8192], P(('attn', 'ffn')), may hold values from -400 to 400
- slot_key_cache: bfloat16 [512, 256, 512], P(('attn', 'ffn')), may hold values from -6 to 6
- slot_value_cache: bfloat16 [512, 256, 512], P(('attn', 'ffn')), may hold values from -16 to 16
- fresh_token_key: bfloat16 [512, 512], P(('attn', 'ffn')), may hold values from -6 to 6
- fresh_token_value: bfloat16 [512, 512], P(('attn', 'ffn')), may hold values from -16 to 16
- lengths: int32 [512], P(('attn', 'ffn')), may hold values from 1 to 256, as said below
- slot_of: int32 [512], replicated, may hold values from 0 to 511, each once
- residual: bfloat16 [512, 16384], P(None, 'attn'), may hold values from -4 to 4
- w_out: bfloat16 [8192, 16384], P('ffn', 'attn'), may hold values from -0.0625 to 0.0625
- norm_gain: bfloat16 [16384], P('attn'), may hold values from 0.099609375 to 1.8984375
- w_gate: bfloat16 [16384, 26624], P('attn', 'ffn'), may hold values from -0.046875 to 0.046875
- w_up: bfloat16 [16384, 26624], P('attn', 'ffn'), may hold values from -0.046875 to 0.046875
- w_down: bfloat16 [26624, 16384], P('ffn', 'attn'), may hold values from -0.0390625 to 0.0390625
Outputs:
- layer_out: bfloat16 [512, 16384], P('ffn', 'attn')
The draws below stay inside these ranges and needn't reach their ends.
Inputs may be any that keep to these rules, and one draw needn't show every extreme that they name: `lengths`: some slot has exactly 256 live positions. `slot_of`: each slot holds exactly one request.
All inputs are finite; a program needn't handle non-finite values.
Results may differ from the reference program's by a relative error of at most 0.011.
Values may be sent and summed in bfloat16 or wider, within the bound.
No kernel may reach another device: no remote copies, remote signals or barrier semaphores. Data moves between devices by JAX's collectives and lax.ppermute only.
A program may use at most 128 MiB of HBM per device.

```python
import jax
import jax.numpy as jnp
from jax import lax

D = 16384
FF = 26624
QUERY_HEADS = 64
KEY_VALUE_HEADS = 4
HEAD_SIZE = 128
SLOT_CAPACITY = 256
REQUEST_TOTAL = 512


def draw_queries(key, part):
    key = jax.random.fold_in(key, 3)
    first_key = jax.random.fold_in(key, 0)
    base = jnp.clip(jax.random.normal(first_key, (REQUEST_TOTAL, QUERY_HEADS * HEAD_SIZE), jnp.float32), -6.0, 6.0)
    return base.astype(jnp.bfloat16)


def draw_lengths(key, part):
    key = jax.random.fold_in(key, 7)
    first_key, second_key = jax.random.split(key)
    drawn = jax.random.randint(first_key, (REQUEST_TOTAL,), 1, SLOT_CAPACITY + 1, jnp.int32)
    chosen = jax.random.randint(second_key, (), 0, REQUEST_TOTAL, jnp.int32)
    return jnp.where(jnp.arange(REQUEST_TOTAL, dtype=jnp.int32) == chosen, SLOT_CAPACITY, drawn).astype(jnp.int32)


def shard_levels(own_key, dims, pieces, low, top_value):
    def one(axis_at, blocks):
        heights = jax.random.uniform(jax.random.fold_in(jax.random.fold_in(own_key, 6), axis_at), (blocks,), jnp.float32, low / len(pieces), top_value / len(pieces))
        return jnp.repeat(jnp.exp(heights), dims[axis_at] // blocks).reshape((-1,) + (1,) * (len(dims) - axis_at - 1))

    loudness = one(*pieces[0])
    for cut in pieces[1:]:
        loudness = loudness * one(*cut)
    return loudness


def scatter_about(rng, extent, deviation, reach, pieces=(), kind=jnp.bfloat16):
    gain = shard_levels(rng, extent, pieces, -0.22, 0.18) if pieces else 1.0
    values = jax.random.normal(rng, extent, jnp.float32) * deviation * gain
    return jnp.minimum(jnp.maximum(values, -reach), reach).astype(kind)


def setup_inputs(seed: int = 0) -> dict:
    splits = jax.random.split(jax.random.key(seed), 14)
    return {
        "queries": draw_queries(jax.random.fold_in(splits[13], 71), 0),
        "slot_key_cache": scatter_about(splits[1], (REQUEST_TOTAL, SLOT_CAPACITY, KEY_VALUE_HEADS * HEAD_SIZE), 1.0, 6.0, ((0, 128),)),
        "slot_value_cache": scatter_about(splits[2], (REQUEST_TOTAL, SLOT_CAPACITY, KEY_VALUE_HEADS * HEAD_SIZE), 3.0, 16.0, ((0, 128),)),
        "fresh_token_key": scatter_about(splits[3], (REQUEST_TOTAL, KEY_VALUE_HEADS * HEAD_SIZE), 1.0, 6.0, ((0, 128),)),
        "fresh_token_value": scatter_about(splits[4], (REQUEST_TOTAL, KEY_VALUE_HEADS * HEAD_SIZE), 3.0, 16.0, ((0, 128),)),
        "lengths": draw_lengths(jax.random.fold_in(splits[13], 71), 0),
        "slot_of": jax.random.permutation(splits[6], REQUEST_TOTAL).astype(jnp.int32),
        "residual": scatter_about(splits[7], (REQUEST_TOTAL, D), 0.5, 4.0, ((1, 8),)),
        "w_out": scatter_about(splits[8], (QUERY_HEADS * HEAD_SIZE, D), (QUERY_HEADS * HEAD_SIZE) ** -0.5, 0.0625, ((0, 16), (1, 8))),
        "norm_gain": jnp.clip(1.0 + 0.18 * jax.random.normal(splits[9], (D,), jnp.float32), 0.099609375, 1.8984375).astype(jnp.bfloat16),
        "w_gate": scatter_about(splits[10], (D, FF), D ** -0.5, 0.046875, ((0, 8), (1, 16))),
        "w_up": scatter_about(splits[11], (D, FF), D ** -0.5, 0.046875, ((0, 8), (1, 16))),
        "w_down": scatter_about(splits[12], (FF, D), FF ** -0.5, 0.0390625, ((0, 16), (1, 8))),
    }


epsilon = 1e-05

def attend(queries, slot_key_cache, slot_value_cache, fresh_token_key, fresh_token_value, lengths):
    request_slot_count = queries.shape[0]
    query_group_width = QUERY_HEADS // KEY_VALUE_HEADS
    query_head_rows = queries.astype(jnp.float32).reshape(request_slot_count, KEY_VALUE_HEADS, query_group_width, HEAD_SIZE)
    stored_keys = slot_key_cache.astype(jnp.float32).reshape(request_slot_count, SLOT_CAPACITY, KEY_VALUE_HEADS, HEAD_SIZE)
    stored_values = slot_value_cache.astype(jnp.float32).reshape(request_slot_count, SLOT_CAPACITY, KEY_VALUE_HEADS, HEAD_SIZE)
    current_key = fresh_token_key.astype(jnp.float32).reshape(request_slot_count, KEY_VALUE_HEADS, HEAD_SIZE)
    current_value = fresh_token_value.astype(jnp.float32).reshape(request_slot_count, KEY_VALUE_HEADS, HEAD_SIZE)
    factor = HEAD_SIZE ** (-0.5)
    scores = jnp.einsum('sgqd,spgd->sgqp', query_head_rows, stored_keys) * factor
    own_score = jnp.einsum('sgqd,sgd->sgq', query_head_rows, current_key) * factor
    live_mask = jnp.arange(SLOT_CAPACITY, dtype=jnp.int32)[None, :] < lengths[:, None]
    scores = jnp.where(live_mask[:, None, None, :], scores, -jnp.inf)
    highest = jnp.maximum(lax.optimization_barrier(jnp.max(scores, axis=-1)), own_score)
    weights = jnp.exp(scores - highest[..., None])
    own_weight = jnp.exp(own_score - highest)
    weight_sum = lax.optimization_barrier(jnp.sum(weights, axis=-1)) + own_weight
    weights_low = lax.optimization_barrier(weights.astype(jnp.bfloat16)).astype(jnp.float32)
    own_low = lax.optimization_barrier(own_weight.astype(jnp.bfloat16)).astype(jnp.float32)
    combined = jnp.einsum('sgqp,spgd->sgqd', weights_low, stored_values)
    combined = combined + own_low[..., None] * current_value[:, :, None, :]
    return (combined / weight_sum[..., None]).reshape(request_slot_count, QUERY_HEADS * HEAD_SIZE).astype(jnp.bfloat16)

def reference(queries, slot_key_cache, slot_value_cache, fresh_token_key, fresh_token_value, lengths, slot_of, residual, w_out, norm_gain, w_gate, w_up, w_down):
    attended = attend(queries, slot_key_cache, slot_value_cache, fresh_token_key, fresh_token_value, lengths)
    ordered = jnp.take(attended, slot_of, axis=0)
    hidden_state = residual.astype(jnp.float32) + jnp.dot(ordered, w_out, preferred_element_type=jnp.float32)
    mean_square = lax.optimization_barrier(jnp.mean(hidden_state * hidden_state, axis=-1))
    normed = (hidden_state * lax.rsqrt(mean_square + epsilon)[:, None] * norm_gain.astype(jnp.float32)).astype(jnp.bfloat16)
    gate_sum = jnp.dot(normed, w_gate, preferred_element_type=jnp.float32)
    up_sum = jnp.dot(normed, w_up, preferred_element_type=jnp.float32)
    hidden = (jax.nn.silu(gate_sum) * up_sum).astype(jnp.bfloat16)
    return (hidden_state + jnp.dot(hidden, w_down, preferred_element_type=jnp.float32)).astype(jnp.bfloat16)
```

```python
import jax
import jax.numpy as jnp
from jax import lax
from jax.sharding import PartitionSpec as P

QUERY_HEADS = 64
KEY_VALUE_HEADS = 4
HEAD_SIZE = 128
SLOT_CAPACITY = 256

epsilon = 1e-05

ATTN, FFN = 8, 16
F32, BF16 = jnp.float32, jnp.bfloat16


def permute(value, move):
    pairs = []
    for a in range(ATTN):
        for f in range(FFN):
            to_a, to_f = move(a, f)
            pairs.append((a * FFN + f, to_a * FFN + to_f))
    return lax.ppermute(value, ("attn", "ffn"), pairs)


def to_core(value):
    return permute(value, lambda a, f: (a, f ^ 1))


def to_x_hi(value):
    return permute(value, lambda a, f: (a, f ^ 2))


def to_x_lo(value):
    return permute(value, lambda a, f: (a ^ 1, f))


def to_y(step):
    return lambda value: permute(value, lambda a, f: (a, (f + 4 * step) % FFN))


def to_z(step):
    return lambda value: permute(value, lambda a, f: ((a + 2 * step) % ATTN, f))


def ring_sum(blocks, to):
    up1 = to(1)(blocks[1:3].reshape((4,) + blocks.shape[2:])[1:3].astype(BF16))
    down1 = to(-1)(blocks[2:4].reshape((4,) + blocks.shape[2:])[1:3].astype(BF16))
    up2 = to(1)((blocks[1, 0] + up1[1].astype(F32)).astype(BF16))
    down2 = to(-1)((blocks[3, 1] + down1[0].astype(F32)).astype(BF16))
    first = blocks[0, 0] + up2.astype(F32) + down1[1].astype(F32)
    second = blocks[0, 1] + up1[0].astype(F32) + down2.astype(F32)
    return first, second


def ring_gather(own, to):
    before = to(1)(own)
    after = to(-1)(own)
    across_first = to(1)(before[0])
    across_second = to(-1)(after[1])
    return jnp.stack([own, after, jnp.stack([across_first, across_second]), before])


def sum_over_ffn(own_half, other_half):
    columns = own_half.shape[1]
    total = own_half + to_core(other_half.astype(BF16)).astype(F32)
    first, second = ring_sum(total.reshape(4, 2, -1, columns), to_y)
    return first + to_x_hi(second.astype(BF16)).astype(F32)


def attend(queries, slot_key_cache, slot_value_cache, fresh_token_key, fresh_token_value, lengths):
    request_slot_count = queries.shape[0]
    query_group_width = QUERY_HEADS // KEY_VALUE_HEADS
    query_head_rows = queries.reshape(
        request_slot_count, KEY_VALUE_HEADS, query_group_width, HEAD_SIZE
    )
    stored_keys = slot_key_cache.reshape(
        request_slot_count, SLOT_CAPACITY, KEY_VALUE_HEADS, HEAD_SIZE
    )
    stored_values = slot_value_cache.reshape(
        request_slot_count, SLOT_CAPACITY, KEY_VALUE_HEADS, HEAD_SIZE
    )
    current_key = fresh_token_key.reshape(request_slot_count, KEY_VALUE_HEADS, HEAD_SIZE)
    current_value = fresh_token_value.astype(F32).reshape(
        request_slot_count, KEY_VALUE_HEADS, HEAD_SIZE
    )
    factor = HEAD_SIZE ** (-0.5)
    scores = (
        jnp.einsum("sgqd,spgd->sgqp", query_head_rows, stored_keys, preferred_element_type=F32)
        * factor
    )
    own_score = (
        jnp.einsum("sgqd,sgd->sgq", query_head_rows, current_key, preferred_element_type=F32)
        * factor
    )
    live_mask = jnp.arange(SLOT_CAPACITY, dtype=jnp.int32)[None, :] < lengths[:, None]
    scores = jnp.where(live_mask[:, None, None, :], scores, -jnp.inf)
    highest = jnp.maximum(jnp.max(scores, axis=-1), own_score)
    weights = jnp.exp(scores - highest[..., None])
    own_weight = jnp.exp(own_score - highest)
    weight_sum = jnp.sum(weights, axis=-1) + own_weight
    own_low = own_weight.astype(BF16).astype(F32)
    combined = jnp.einsum(
        "sgqp,spgd->sgqd", weights.astype(BF16), stored_values, preferred_element_type=F32
    )
    combined = combined + own_low[..., None] * current_value[:, :, None, :]
    return (
        (combined / weight_sum[..., None])
        .reshape(request_slot_count, QUERY_HEADS * HEAD_SIZE)
        .astype(BF16)
    )


def local(
    queries,
    slot_key_cache,
    slot_value_cache,
    fresh_token_key,
    fresh_token_value,
    lengths,
    slot_of,
    residual,
    w_out,
    norm_gain,
    w_gate,
    w_up,
    w_down,
):
    a, f = lax.axis_index("attn"), lax.axis_index("ffn")
    z, x_lo = a // 2, a % 2
    y, x_hi, core = f // 4, (f // 2) % 2, f % 2
    slots = queries.shape[0]
    features = w_out.shape[0]
    width = w_out.shape[1]
    rows = residual.shape[0]
    share = rows // FFN
    batch = rows // ATTN
    width_total = width * ATTN

    attended = attend(
        queries, slot_key_cache, slot_value_cache, fresh_token_key, fresh_token_value, lengths
    )

    step = jnp.arange(FFN, dtype=jnp.int32)
    step_core, step_y, step_x = step // 8, (step // 2) % 4, step % 2
    partner = ((y + step_y) % 4) * 4 + (x_hi ^ step_x) * 2 + (core ^ step_core)

    parts = attended.reshape(slots, FFN, features).transpose(1, 0, 2)
    parts = jnp.take(parts, partner, axis=0).reshape(2, 4, 2, slots * features)
    parts = jnp.stack([parts[0], to_core(parts[1])])
    parts = jnp.stack([parts[:, :, 0], to_x_hi(parts[:, :, 1])])
    parts = jnp.stack(
        [parts[:, :, 0]] + [to_y(s)(parts[:, :, s]) for s in (1, 2, 3)]
    )
    parts = parts.reshape(2, FFN // 2, slots * features)
    parts = jnp.stack([parts, to_x_lo(parts)])
    parts = ring_gather(parts, to_z)
    held = parts.reshape(rows, features)

    wanted = (partner[:, None] * share + jnp.arange(share, dtype=jnp.int32)).reshape(rows)
    slot = jnp.take(slot_of, wanted)
    slot_a, slot_f, slot_i = slot // (FFN * slots), (slot // slots) % FFN, slot % slots
    place = (slot_a // 2 - z) % 4
    place = place * 2 + ((slot_a % 2) ^ x_lo)
    place = place * 4 + (y - slot_f // 4) % 4
    place = place * 2 + (((slot_f // 2) % 2) ^ x_hi)
    place = place * 2 + ((slot_f % 2) ^ core)
    place = place * slots + slot_i
    choice = (place[:, None] == jnp.arange(rows, dtype=jnp.int32)[None, :]).astype(BF16)
    ordered = jnp.dot(choice, held, preferred_element_type=F32).astype(BF16)

    half = rows // 2
    summed = sum_over_ffn(
        jnp.dot(ordered[:half], w_out, preferred_element_type=F32),
        jnp.dot(ordered[half:], w_out, preferred_element_type=F32),
    )
    kept = lax.dynamic_slice_in_dim(residual, f * share, share, 0).astype(F32)
    hidden_state = kept + summed

    squares = jnp.sum(hidden_state * hidden_state, axis=-1)
    squares = squares + to_x_lo(squares)
    squares = squares + to_z(1)(squares) + to_z(2)(squares) + to_z(3)(squares)
    gain = norm_gain.astype(F32)
    normed = (
        hidden_state * lax.rsqrt(squares / width_total + epsilon)[:, None] * gain
    ).astype(BF16)

    normed = jnp.stack([normed, to_x_hi(normed)])
    normed = ring_gather(normed, to_y)
    normed = jnp.stack([normed, to_core(normed)])

    ahead = jnp.arange(ATTN, dtype=jnp.int32)
    order = ((z + ahead // 2) % 4) * 2 + (x_lo ^ (ahead % 2))
    back = ((ahead // 2 - z) % 4) * 2 + (x_lo ^ (ahead % 2))
    normed = jnp.take(normed.reshape(ATTN, batch, width), order, axis=0).reshape(rows, width)

    up = jnp.dot(normed, w_up, preferred_element_type=F32).reshape(4, 2, batch, -1)
    gate = jnp.dot(normed, w_gate, preferred_element_type=F32).reshape(4, 2, batch, -1)
    units = w_up.shape[1]
    up = up[:, 0] + to_x_lo(up[:, 1].astype(BF16)).astype(F32)
    gate, gate_across = ring_sum(gate, to_z)
    gate = gate + to_x_lo(gate_across.astype(BF16)).astype(F32)
    up = jnp.concatenate(ring_sum(up.reshape(4, 2, batch // 2, units), to_z), axis=0)
    hidden = (jax.nn.silu(gate) * up).astype(BF16)

    cut = 128 * (units // 256)
    left, right = hidden[:, :cut], hidden[:, cut:]
    left = ring_gather(jnp.stack([left, to_x_lo(left)]), to_z)
    right = ring_gather(right.reshape(2, batch // 2, -1), to_z).reshape(4, batch, -1)
    right = jnp.stack([right, to_x_lo(right)], axis=1)
    hidden = jnp.concatenate([left, right], axis=-1).reshape(ATTN, batch, units)
    hidden = jnp.take(hidden, back, axis=0).reshape(rows, units)

    down_out = sum_over_ffn(
        jnp.dot(hidden[:half], w_down, preferred_element_type=F32),
        jnp.dot(hidden[half:], w_down, preferred_element_type=F32),
    )
    return (hidden_state + down_out).astype(BF16)


def solution(mesh):
    in_specs = (
        P(("attn", "ffn"), None),
        P(("attn", "ffn"), None, None),
        P(("attn", "ffn"), None, None),
        P(("attn", "ffn"), None),
        P(("attn", "ffn"), None),
        P(("attn", "ffn")),
        P(),
        P(None, "attn"),
        P("ffn", "attn"),
        P("attn"),
        P("attn", "ffn"),
        P("attn", "ffn"),
        P("ffn", "attn"),
    )
    out_specs = P("ffn", "attn")
    return jax.shard_map(local, mesh=mesh, in_specs=in_specs, out_specs=out_specs, check_vma=False)
```

```python
import functools

import jax
import jax.numpy as jnp
from jax import lax
from jax.experimental import pallas as pl
from jax.experimental.pallas import tpu as pltpu
from jax.sharding import PartitionSpec as P

QUERY_HEADS = 64
KEY_VALUE_HEADS = 4
HEAD_SIZE = 128
SLOT_CAPACITY = 256

epsilon = 1e-05

F32, BF16 = jnp.float32, jnp.bfloat16
LANES = 128
FLOWS = 3

ATTN, FFN = 8, 16
SAME_CORE = [[2 * chip + core for chip in range(FFN // 2)] for core in range(2)]


def over_core(value):
    pairs = [(n, n ^ 1) for n in range(FFN)]
    return lax.ppermute(value, "ffn", pairs)


def over_chips(blocks):
    return lax.all_to_all(blocks, "ffn", 0, 0, tiled=True, axis_index_groups=SAME_CORE)


AXES = ((2, 4, 1), (4, 1, 2))
ORDERS = ((0, 1, 2), (1, 2, 0), (2, 0, 1))


def gray(place):
    return place ^ ((place & 4) >> 1)


def over_cube(value, axis):
    pairs = []
    for a in range(ATTN):
        for f in range(FFN):
            to_a = gray(gray(a) ^ AXES[f & 1][axis])
            pairs.append((a * FFN + f, to_a * FFN + f))
    return lax.ppermute(value, ("attn", "ffn"), pairs)


def cube_sum(sent, kept, order):
    for axis in order:
        total = kept.astype(F32) + over_cube(sent, axis).astype(F32)
        middle = total.shape[0] // 2
        sent, kept = total[:middle].astype(BF16), total[middle:]
    return total[0]


def cube_gather(own, order):
    own = own[None]
    for axis in order[:0:-1]:
        own = jnp.concatenate([over_cube(own, axis), own])
    return over_cube(own, order[0]), own


VMEM = pl.BlockSpec(memory_space=pltpu.VMEM)
SMEM = pl.BlockSpec(memory_space=pltpu.SMEM)
HBM = pl.BlockSpec(memory_space=pl.ANY)
TILE = 256
VMEM_LIMIT = 24 * 2**20


def load_kernel(count, *refs):
    arrived = refs[-1]
    copies = [
        pltpu.make_async_copy(refs[n], refs[count + n], arrived.at[n]) for n in range(count)
    ]
    for copy in copies:
        copy.start()
    for copy in copies:
        copy.wait()


def load(*arrays):
    count = len(arrays)
    return pl.pallas_call(
        functools.partial(load_kernel, count),
        out_shape=[jax.ShapeDtypeStruct(array.shape, array.dtype) for array in arrays],
        in_specs=[HBM] * count,
        out_specs=[VMEM] * count,
        scratch_shapes=[pltpu.SemaphoreType.DMA((count,))],
        compiler_params=pltpu.CompilerParams(vmem_limit_bytes=VMEM_LIMIT),
        cost_estimate=pl.CostEstimate(
            flops=0,
            bytes_accessed=sum(2 * array.size * array.dtype.itemsize for array in arrays),
            transcendentals=0,
        ),
    )(*arrays)


def gate_up_kernel(cut, place, x, w_gate, w_up, sent, kept, placed):
    batch = sent.shape[1]

    def store(value, at):
        for block in range(ATTN):
            part = value[block * batch : (block + 1) * batch]
            placed[place[block], :, at : at + value.shape[1]] = part

    at = 0
    for weights in (w_gate, w_up):
        for start in range(cut.start, cut.stop, TILE):
            columns = slice(start, min(start + TILE, cut.stop))
            product = jnp.dot(x[...], weights[:, columns], preferred_element_type=F32)
            store(product.astype(BF16), at)
            at += columns.stop - columns.start
    sent[...] = placed[: ATTN // 2]
    kept[...] = placed[ATTN // 2 :]


def first_gate_up_kernel(cut, place, own, other, w_gate, w_up, sent, kept, x, placed):
    depth = x.shape[1]
    half = own.shape[0]
    x[:half] = own[:, :depth]
    x[half:] = other[:, :depth]
    batch = sent.shape[1]
    for block in range(ATTN):
        rows, row = (own, block * batch) if block < ATTN // 2 else (other, block * batch - half)
        placed[place[block], :, 2 * (cut.stop - cut.start) :] = rows[row : row + batch, depth:]
    gate_up_kernel(cut, place, x, w_gate, w_up, sent, kept, placed)


def gate_up(place, x, w_gate, w_up, cut):
    depth = w_gate.shape[0]
    rows = sum(part.shape[0] for part in x)
    width = 2 * (cut.stop - cut.start) + x[0].shape[1] - depth
    half = jax.ShapeDtypeStruct((ATTN // 2, rows // ATTN, width), BF16)
    whole = [jax.ShapeDtypeStruct((rows, depth), BF16)] * (len(x) - 1)
    body = first_gate_up_kernel if whole else gate_up_kernel
    return pl.pallas_call(
        functools.partial(body, cut),
        out_shape=[half, half] + whole,
        in_specs=[SMEM] + [VMEM] * (len(x) + 2),
        out_specs=[VMEM] * (2 + len(whole)),
        scratch_shapes=[pltpu.VMEM((ATTN, rows // ATTN, width), BF16)],
        compiler_params=pltpu.CompilerParams(vmem_limit_bytes=VMEM_LIMIT),
        cost_estimate=pl.CostEstimate(
            flops=2 * rows * depth * width,
            bytes_accessed=2 * depth * width + 2 * rows * depth,
            transcendentals=0,
        ),
    )(place, *x, w_gate, w_up)


def down_kernel(place, *refs):
    parts, (w_down, own, other, hidden) = refs[: 2 * FLOWS], refs[2 * FLOWS :]
    at = 0
    for flow in range(FLOWS):
        batch, width = parts[2 * flow].shape[1:]
        for block in range(ATTN):
            part = parts[2 * flow + block // (ATTN // 2)][block % (ATTN // 2)]
            row = pl.multiple_of(place[flow, block] * batch, batch)
            hidden[pl.ds(row, batch), at : at + width] = part
        at += width
    half = own.shape[0]
    for start in range(0, own.shape[1], TILE):
        columns = slice(start, start + TILE)
        product = jnp.dot(hidden[...], w_down[:, columns], preferred_element_type=F32)
        own[:, columns] = product[:half]
        other[:, columns] = product[half:].astype(BF16)


def down(place, parts, w_down):
    units, width = w_down.shape
    rows = ATTN * parts[0].shape[1]
    return pl.pallas_call(
        down_kernel,
        out_shape=(
            jax.ShapeDtypeStruct((rows // 2, width), F32),
            jax.ShapeDtypeStruct((rows // 2, width), BF16),
        ),
        in_specs=[SMEM] + [VMEM] * (2 * FLOWS) + [VMEM],
        out_specs=(VMEM, VMEM),
        scratch_shapes=[pltpu.VMEM((rows, units), BF16)],
        compiler_params=pltpu.CompilerParams(vmem_limit_bytes=VMEM_LIMIT),
        cost_estimate=pl.CostEstimate(
            flops=2 * rows * units * width,
            bytes_accessed=2 * units * width + 2 * rows * units + 3 * rows * width,
            transcendentals=0,
        ),
    )(place, *parts, w_down)


def copies(value):
    return lax.optimization_barrier(jnp.broadcast_to(value, (8,) + value.shape))


def attend_kernel(lengths, queries, keys, values, own_key, own_value, out, heads, held, arrived, done):
    slots = queries.shape[0]
    group = QUERY_HEADS // KEY_VALUE_HEADS
    features = out.shape[2]
    fetches = []
    for slot in range(slots):
        fetches.append(
            (
                pltpu.make_async_copy(keys.at[slot], held.at[0, slot], arrived.at[0, slot]),
                pltpu.make_async_copy(values.at[slot], held.at[1, slot], arrived.at[1, slot]),
            )
        )
    for pair in fetches:
        for fetch in pair:
            fetch.start()
    wide = queries[...].astype(F32)
    for slot in range(slots):
        for head in range(QUERY_HEADS):
            heads[slot, head : head + 1] = wide[
                slot : slot + 1, head * HEAD_SIZE : (head + 1) * HEAD_SIZE
            ]
    factor = HEAD_SIZE ** (-0.5)
    position = lax.broadcasted_iota(jnp.int32, (QUERY_HEADS, SLOT_CAPACITY), 1)
    for slot in range(slots):
        for fetch in fetches[slot]:
            fetch.wait()
        query = heads[slot]
        own_score, scores = [], []
        for kv in range(KEY_VALUE_HEADS):
            at = slice(kv * HEAD_SIZE, (kv + 1) * HEAD_SIZE)
            part = query[kv * group : (kv + 1) * group]
            scores.append(
                lax.dot_general(
                    part.astype(BF16),
                    held[0, slot, :, at],
                    (((1,), (1,)), ((), ())),
                    preferred_element_type=F32,
                )
            )
            key = own_key[slot : slot + 1, at].astype(F32)
            own_score.append(jnp.sum(part * key, axis=-1, keepdims=True) * factor)
        scores = jnp.where(position < lengths[slot], jnp.concatenate(scores) * factor, -jnp.inf)
        own_score = jnp.concatenate(own_score)
        highest = jnp.maximum(jnp.max(scores, axis=-1, keepdims=True), own_score)
        weights = jnp.exp(scores - highest)
        own_weight = jnp.exp(own_score - highest)
        weight_sum = jnp.sum(weights, axis=-1, keepdims=True) + own_weight
        own_low = own_weight.astype(BF16).astype(F32)
        for kv in range(KEY_VALUE_HEADS):
            at = slice(kv * HEAD_SIZE, (kv + 1) * HEAD_SIZE)
            own_heads = slice(kv * group, (kv + 1) * group)
            combined = jnp.dot(
                weights[own_heads].astype(BF16), held[1, slot, :, at], preferred_element_type=F32
            )
            value = own_value[slot : slot + 1, at].astype(F32)
            combined = (combined + own_low[own_heads] * value) / weight_sum[own_heads]
            for n in range(group):
                first = (kv * group + n) * HEAD_SIZE
                to = first % features
                done[first // features, slot : slot + 1, to : to + HEAD_SIZE] = combined[n : n + 1]
    whole = done[...].astype(BF16)
    for device in range(ATTN):
        out[device * FFN : (device + 1) * FFN] = whole


def attend(queries, slot_key_cache, slot_value_cache, fresh_token_key, fresh_token_value, lengths):
    slots, features = queries.shape[0], QUERY_HEADS * HEAD_SIZE // FFN
    return pl.pallas_call(
        attend_kernel,
        out_shape=jax.ShapeDtypeStruct((ATTN * FFN, slots, features), BF16),
        in_specs=[SMEM, VMEM, HBM, HBM, VMEM, VMEM],
        out_specs=VMEM,
        scratch_shapes=[
            pltpu.VMEM((slots, QUERY_HEADS, HEAD_SIZE), F32),
            pltpu.VMEM((2,) + slot_key_cache.shape, BF16),
            pltpu.SemaphoreType.DMA((2, slots)),
            pltpu.VMEM((FFN, slots, features), F32),
        ],
        compiler_params=pltpu.CompilerParams(vmem_limit_bytes=58 * 2**20),
        cost_estimate=pl.CostEstimate(
            flops=4 * queries.size * SLOT_CAPACITY,
            bytes_accessed=4 * slot_key_cache.size,
            transcendentals=slots * QUERY_HEADS * SLOT_CAPACITY,
        ),
    )(lengths, queries, slot_key_cache, slot_value_cache, fresh_token_key, fresh_token_value)


def local(
    queries,
    slot_key_cache,
    slot_value_cache,
    fresh_token_key,
    fresh_token_value,
    lengths,
    slot_of,
    residual,
    w_out,
    norm_gain,
    w_gate,
    w_up,
    w_down,
):
    f = lax.axis_index("ffn")
    core = f % 2
    slots = queries.shape[0]
    features, width = w_out.shape
    units = w_up.shape[1]
    rows = residual.shape[0]
    share, batch, half = rows // FFN, rows // ATTN, rows // 2
    width_total = width * ATTN

    parts = attend(
        queries, slot_key_cache, slot_value_cache, fresh_token_key, fresh_token_value, lengths
    )
    held = lax.all_to_all(parts, ("attn", "ffn"), 0, 0, tiled=True).reshape(rows, features)

    by_core = slot_of.reshape(FFN // 2, 2, share)
    swapped = jnp.where(core == 0, by_core, by_core[:, ::-1])
    wanted = swapped.transpose(1, 0, 2).reshape(rows)
    choice = (wanted[:, None] == jnp.arange(rows, dtype=jnp.int32)[None, :]).astype(BF16)
    ordered = jnp.dot(choice, held, preferred_element_type=F32).astype(BF16)
    kept = lax.dynamic_slice_in_dim(residual, f * share, share, 0).astype(F32)

    def sum_over_cores(own, other):
        total = own + over_core(other).astype(F32)
        return total.astype(BF16).reshape(FFN // 2, share, width)

    def sum_over_chips(blocks):
        return jnp.sum(over_chips(blocks).astype(F32), axis=0)

    other = jnp.dot(ordered[half:], w_out, preferred_element_type=F32).astype(BF16)
    blocks = sum_over_cores(jnp.dot(ordered[:half], w_out, preferred_element_type=F32), other)
    blocks, *weights = lax.optimization_barrier((blocks, w_gate, w_up, w_down))
    w_gate, w_up, w_down = load(*weights)
    state = kept + sum_over_chips(blocks)
    squares = jnp.sum(state * state, axis=-1, keepdims=True)
    scaled = jnp.concatenate(
        [state * norm_gain.astype(F32), jnp.broadcast_to(squares, (share, LANES))], axis=1
    )
    scaled = over_chips(copies(scaled.astype(BF16))).reshape(half, width + LANES)
    x = [scaled, over_core(scaled)]

    eight = jnp.arange(ATTN, dtype=jnp.int32)
    attn_at = gray(lax.axis_index("attn"))

    def masks(flow):
        return [jnp.where(core == 0, AXES[0][axis], AXES[1][axis]) for axis in ORDERS[flow]]

    def place_of(flow):
        flipped = attn_at ^ gray(eight)
        bits = [((flipped & mask) == 0).astype(jnp.int32) for mask in masks(flow)]
        return bits[0] * 4 + bits[1] * 2 + bits[2]

    def block_at(flow):
        flips = [(1 - ((eight >> (2 - n)) & 1)) * mask for n, mask in enumerate(masks(flow))]
        return gray(attn_at ^ flips[0] ^ flips[1] ^ flips[2])

    tiles = units // LANES
    edges = [tiles * flow // FLOWS * LANES for flow in range(FLOWS + 1)]
    sums = []
    for flow in range(FLOWS):
        sent, kept, *whole = gate_up(
            place_of(flow), x, w_gate, w_up, slice(edges[flow], edges[flow + 1])
        )
        x = whole or x
        sums.append(cube_sum(sent, kept, ORDERS[flow]))
    scale = lax.rsqrt(sums[0][:, -1:] / width_total + epsilon)
    hidden = []
    for flow, both in enumerate(sums):
        size = edges[flow + 1] - edges[flow]
        gate, up = both[:, :size] * scale, both[:, size : 2 * size] * scale
        hidden += cube_gather((jax.nn.silu(gate) * up).astype(BF16), ORDERS[flow])
    blocks = jnp.stack([block_at(flow) for flow in range(FLOWS)])
    products = down(blocks, hidden, w_down)
    return (state + sum_over_chips(sum_over_cores(*products))).astype(BF16)


def solution(mesh):
    in_specs = (
        P(("attn", "ffn"), None),
        P(("attn", "ffn"), None, None),
        P(("attn", "ffn"), None, None),
        P(("attn", "ffn"), None),
        P(("attn", "ffn"), None),
        P(("attn", "ffn")),
        P(),
        P(None, "attn"),
        P("ffn", "attn"),
        P("attn"),
        P("attn", "ffn"),
        P("attn", "ffn"),
        P("ffn", "attn"),
    )
    out_specs = P("ffn", "attn")
    return jax.shard_map(local, mesh=mesh, in_specs=in_specs, out_specs=out_specs, check_vma=False)
```

```python
import functools

import jax
import jax.numpy as jnp
from jax import lax
from jax.experimental import pallas as pl
from jax.experimental.pallas import tpu as pltpu
from jax.sharding import PartitionSpec as P

QUERY_HEADS = 64
KEY_VALUE_HEADS = 4
HEAD_SIZE = 128
SLOT_CAPACITY = 256

epsilon = 1e-05

F32, BF16 = jnp.float32, jnp.bfloat16
LANES = 128
FLOWS = 3

ATTN, FFN = 8, 16
SAME_CORE = [[2 * chip + core for chip in range(FFN // 2)] for core in range(2)]


def over_core(value):
    pairs = [(n, n ^ 1) for n in range(FFN)]
    return lax.ppermute(value, "ffn", pairs)


def over_chips(blocks):
    return lax.all_to_all(blocks, "ffn", 0, 0, tiled=True, axis_index_groups=SAME_CORE)


AXES = ((2, 4, 1), (4, 1, 2))
ORDERS = ((0, 1, 2), (1, 2, 0), (2, 0, 1))


def gray(place):
    return place ^ ((place & 4) >> 1)


def over_cube(value, axis):
    pairs = []
    for a in range(ATTN):
        for f in range(FFN):
            to_a = gray(gray(a) ^ AXES[f & 1][axis])
            pairs.append((a * FFN + f, to_a * FFN + f))
    return lax.ppermute(value, ("attn", "ffn"), pairs)


def cube_sum(sent, kept, order):
    for axis in order:
        total = kept.astype(F32) + over_cube(sent, axis).astype(F32)
        middle = total.shape[0] // 2
        sent, kept = total[:middle].astype(BF16), total[middle:]
    return total[0]


def cube_gather(own, order):
    own = own[None]
    for axis in order[:0:-1]:
        own = jnp.concatenate([over_cube(own, axis), own])
    return over_cube(own, order[0]), own


VMEM = pl.BlockSpec(memory_space=pltpu.VMEM)
SMEM = pl.BlockSpec(memory_space=pltpu.SMEM)
HBM = pl.BlockSpec(memory_space=pl.ANY)
TILE = 256
VMEM_LIMIT = 24 * 2**20


def load_kernel(count, *refs):
    arrived = refs[-1]
    copies = [
        pltpu.make_async_copy(refs[n], refs[count + n], arrived.at[n]) for n in range(count)
    ]
    for copy in copies:
        copy.start()
    for copy in copies:
        copy.wait()


def load(*arrays):
    count = len(arrays)
    return pl.pallas_call(
        functools.partial(load_kernel, count),
        out_shape=[jax.ShapeDtypeStruct(array.shape, array.dtype) for array in arrays],
        in_specs=[HBM] * count,
        out_specs=[VMEM] * count,
        scratch_shapes=[pltpu.SemaphoreType.DMA((count,))],
        compiler_params=pltpu.CompilerParams(vmem_limit_bytes=VMEM_LIMIT),
        cost_estimate=pl.CostEstimate(
            flops=0,
            bytes_accessed=sum(2 * array.size * array.dtype.itemsize for array in arrays),
            transcendentals=0,
        ),
    )(*arrays)


def gate_up_kernel(cut, place, x, w_gate, w_up, sent, kept, placed):
    batch = sent.shape[1]

    def store(value, at):
        for block in range(ATTN):
            part = value[block * batch : (block + 1) * batch]
            placed[place[block], :, at : at + value.shape[1]] = part

    at = 0
    for weights in (w_gate, w_up):
        for start in range(cut.start, cut.stop, TILE):
            columns = slice(start, min(start + TILE, cut.stop))
            product = jnp.dot(x[...], weights[:, columns], preferred_element_type=F32)
            store(product.astype(BF16), at)
            at += columns.stop - columns.start
    sent[...] = placed[: ATTN // 2]
    kept[...] = placed[ATTN // 2 :]


def first_gate_up_kernel(cut, place, own, other, w_gate, w_up, sent, kept, x, placed):
    depth = x.shape[1]
    half = own.shape[0]
    x[:half] = own[:, :depth]
    x[half:] = other[:, :depth]
    batch = sent.shape[1]
    for block in range(ATTN):
        rows, row = (own, block * batch) if block < ATTN // 2 else (other, block * batch - half)
        placed[place[block], :, 2 * (cut.stop - cut.start) :] = rows[row : row + batch, depth:]
    gate_up_kernel(cut, place, x, w_gate, w_up, sent, kept, placed)


def gate_up(place, x, w_gate, w_up, cut):
    depth = w_gate.shape[0]
    rows = sum(part.shape[0] for part in x)
    width = 2 * (cut.stop - cut.start) + x[0].shape[1] - depth
    half = jax.ShapeDtypeStruct((ATTN // 2, rows // ATTN, width), BF16)
    whole = [jax.ShapeDtypeStruct((rows, depth), BF16)] * (len(x) - 1)
    body = first_gate_up_kernel if whole else gate_up_kernel
    return pl.pallas_call(
        functools.partial(body, cut),
        out_shape=[half, half] + whole,
        in_specs=[SMEM] + [VMEM] * (len(x) + 2),
        out_specs=[VMEM] * (2 + len(whole)),
        scratch_shapes=[pltpu.VMEM((ATTN, rows // ATTN, width), BF16)],
        compiler_params=pltpu.CompilerParams(vmem_limit_bytes=VMEM_LIMIT),
        cost_estimate=pl.CostEstimate(
            flops=2 * rows * depth * width,
            bytes_accessed=2 * depth * width + 2 * rows * depth,
            transcendentals=0,
        ),
    )(place, *x, w_gate, w_up)


def down_kernel(place, *refs):
    parts, (w_down, own, other, hidden) = refs[: 2 * FLOWS], refs[2 * FLOWS :]
    at = 0
    for flow in range(FLOWS):
        batch, width = parts[2 * flow].shape[1:]
        for block in range(ATTN):
            part = parts[2 * flow + block // (ATTN // 2)][block % (ATTN // 2)]
            row = pl.multiple_of(place[flow, block] * batch, batch)
            hidden[pl.ds(row, batch), at : at + width] = part
        at += width
    half = own.shape[0]
    for start in range(0, own.shape[1], TILE):
        columns = slice(start, start + TILE)
        product = jnp.dot(hidden[...], w_down[:, columns], preferred_element_type=F32)
        own[:, columns] = product[:half]
        other[:, columns] = product[half:].astype(BF16)


def down(place, parts, w_down):
    units, width = w_down.shape
    rows = ATTN * parts[0].shape[1]
    return pl.pallas_call(
        down_kernel,
        out_shape=(
            jax.ShapeDtypeStruct((rows // 2, width), F32),
            jax.ShapeDtypeStruct((rows // 2, width), BF16),
        ),
        in_specs=[SMEM] + [VMEM] * (2 * FLOWS) + [VMEM],
        out_specs=(VMEM, VMEM),
        scratch_shapes=[pltpu.VMEM((rows, units), BF16)],
        compiler_params=pltpu.CompilerParams(vmem_limit_bytes=VMEM_LIMIT),
        cost_estimate=pl.CostEstimate(
            flops=2 * rows * units * width,
            bytes_accessed=2 * units * width + 2 * rows * units + 3 * rows * width,
            transcendentals=0,
        ),
    )(place, *parts, w_down)


def copies(value):
    return lax.optimization_barrier(jnp.broadcast_to(value, (8,) + value.shape))


def attend_kernel(lengths, queries, keys, values, own_key, own_value, out, heads, held, arrived, done):
    slots = queries.shape[0]
    group = QUERY_HEADS // KEY_VALUE_HEADS
    features = out.shape[2]
    fetches = []
    for slot in range(slots):
        fetches.append(
            (
                pltpu.make_async_copy(keys.at[slot], held.at[0, slot], arrived.at[0, slot]),
                pltpu.make_async_copy(values.at[slot], held.at[1, slot], arrived.at[1, slot]),
            )
        )
    for pair in fetches:
        for fetch in pair:
            fetch.start()
    wide = queries[...].astype(F32)
    for slot in range(slots):
        for head in range(QUERY_HEADS):
            heads[slot, head : head + 1] = wide[
                slot : slot + 1, head * HEAD_SIZE : (head + 1) * HEAD_SIZE
            ]
    factor = HEAD_SIZE ** (-0.5)
    position = lax.broadcasted_iota(jnp.int32, (QUERY_HEADS, SLOT_CAPACITY), 1)
    for slot in range(slots):
        for fetch in fetches[slot]:
            fetch.wait()
        query = heads[slot]
        own_score, scores = [], []
        for kv in range(KEY_VALUE_HEADS):
            at = slice(kv * HEAD_SIZE, (kv + 1) * HEAD_SIZE)
            part = query[kv * group : (kv + 1) * group]
            scores.append(
                lax.dot_general(
                    part.astype(BF16),
                    held[0, slot, :, at],
                    (((1,), (1,)), ((), ())),
                    preferred_element_type=F32,
                )
            )
            key = own_key[slot : slot + 1, at].astype(F32)
            own_score.append(jnp.sum(part * key, axis=-1, keepdims=True) * factor)
        scores = jnp.where(position < lengths[slot], jnp.concatenate(scores) * factor, -jnp.inf)
        own_score = jnp.concatenate(own_score)
        highest = jnp.maximum(jnp.max(scores, axis=-1, keepdims=True), own_score)
        weights = jnp.exp(scores - highest)
        own_weight = jnp.exp(own_score - highest)
        weight_sum = jnp.sum(weights, axis=-1, keepdims=True) + own_weight
        own_low = own_weight.astype(BF16).astype(F32)
        for kv in range(KEY_VALUE_HEADS):
            at = slice(kv * HEAD_SIZE, (kv + 1) * HEAD_SIZE)
            own_heads = slice(kv * group, (kv + 1) * group)
            combined = jnp.dot(
                weights[own_heads].astype(BF16), held[1, slot, :, at], preferred_element_type=F32
            )
            value = own_value[slot : slot + 1, at].astype(F32)
            combined = (combined + own_low[own_heads] * value) / weight_sum[own_heads]
            for n in range(group):
                first = (kv * group + n) * HEAD_SIZE
                to = first % features
                done[first // features, slot : slot + 1, to : to + HEAD_SIZE] = combined[n : n + 1]
    whole = done[...].astype(BF16)
    for device in range(ATTN):
        out[device * FFN : (device + 1) * FFN] = whole


def attend(queries, slot_key_cache, slot_value_cache, fresh_token_key, fresh_token_value, lengths):
    slots, features = queries.shape[0], QUERY_HEADS * HEAD_SIZE // FFN
    return pl.pallas_call(
        attend_kernel,
        out_shape=jax.ShapeDtypeStruct((ATTN * FFN, slots, features), BF16),
        in_specs=[SMEM, VMEM, HBM, HBM, VMEM, VMEM],
        out_specs=VMEM,
        scratch_shapes=[
            pltpu.VMEM((slots, QUERY_HEADS, HEAD_SIZE), F32),
            pltpu.VMEM((2,) + slot_key_cache.shape, BF16),
            pltpu.SemaphoreType.DMA((2, slots)),
            pltpu.VMEM((FFN, slots, features), F32),
        ],
        compiler_params=pltpu.CompilerParams(vmem_limit_bytes=58 * 2**20),
        cost_estimate=pl.CostEstimate(
            flops=4 * queries.size * SLOT_CAPACITY,
            bytes_accessed=4 * slot_key_cache.size,
            transcendentals=slots * QUERY_HEADS * SLOT_CAPACITY,
        ),
    )(lengths, queries, slot_key_cache, slot_value_cache, fresh_token_key, fresh_token_value)


def local(
    queries,
    slot_key_cache,
    slot_value_cache,
    fresh_token_key,
    fresh_token_value,
    lengths,
    slot_of,
    residual,
    w_out,
    norm_gain,
    w_gate,
    w_up,
    w_down,
):
    f = lax.axis_index("ffn")
    core = f % 2
    slots = queries.shape[0]
    features, width = w_out.shape
    units = w_up.shape[1]
    rows = residual.shape[0]
    share, batch, half = rows // FFN, rows // ATTN, rows // 2
    width_total = width * ATTN

    parts = attend(
        queries, slot_key_cache, slot_value_cache, fresh_token_key, fresh_token_value, lengths
    )
    held = lax.all_to_all(parts, ("attn", "ffn"), 0, 0, tiled=True).reshape(rows, features)

    by_core = slot_of.reshape(FFN // 2, 2, share)
    swapped = jnp.where(core == 0, by_core, by_core[:, ::-1])
    wanted = swapped.transpose(1, 0, 2).reshape(rows)
    choice = (wanted[:, None] == jnp.arange(rows, dtype=jnp.int32)[None, :]).astype(BF16)
    ordered = jnp.dot(choice, held, preferred_element_type=F32).astype(BF16)
    kept = lax.dynamic_slice_in_dim(residual, f * share, share, 0).astype(F32)

    def sum_over_cores(own, other):
        total = own + over_core(other).astype(F32)
        return total.astype(BF16).reshape(FFN // 2, share, width)

    def sum_over_chips(blocks):
        return jnp.sum(over_chips(blocks).astype(F32), axis=0)

    other = jnp.dot(ordered[half:], w_out, preferred_element_type=F32).astype(BF16)
    blocks = sum_over_cores(jnp.dot(ordered[:half], w_out, preferred_element_type=F32), other)
    blocks, *weights = lax.optimization_barrier((blocks, w_gate, w_up))
    w_gate, w_up = load(*weights)
    state = kept + sum_over_chips(blocks)
    squares = jnp.sum(state * state, axis=-1, keepdims=True)
    scaled = jnp.concatenate(
        [state * norm_gain.astype(F32), jnp.broadcast_to(squares, (share, LANES))], axis=1
    )
    scaled = over_chips(copies(scaled.astype(BF16))).reshape(half, width + LANES)
    x = [scaled, over_core(scaled)]

    eight = jnp.arange(ATTN, dtype=jnp.int32)
    attn_at = gray(lax.axis_index("attn"))

    def masks(flow):
        return [jnp.where(core == 0, AXES[0][axis], AXES[1][axis]) for axis in ORDERS[flow]]

    def place_of(flow):
        flipped = attn_at ^ gray(eight)
        bits = [((flipped & mask) == 0).astype(jnp.int32) for mask in masks(flow)]
        return bits[0] * 4 + bits[1] * 2 + bits[2]

    def block_at(flow):
        flips = [(1 - ((eight >> (2 - n)) & 1)) * mask for n, mask in enumerate(masks(flow))]
        return gray(attn_at ^ flips[0] ^ flips[1] ^ flips[2])

    tiles = units // LANES
    edges = [tiles * flow // FLOWS * LANES for flow in range(FLOWS + 1)]
    sums = []
    for flow in range(FLOWS):
        sent, kept, *whole = gate_up(
            place_of(flow), x, w_gate, w_up, slice(edges[flow], edges[flow + 1])
        )
        x = whole or x
        sums.append(cube_sum(sent, kept, ORDERS[flow]))
    sums[0], w_down = lax.optimization_barrier((sums[0], w_down))
    (w_down,) = load(w_down)
    scale = lax.rsqrt(sums[0][:, -1:] / width_total + epsilon)
    hidden = []
    for flow, both in enumerate(sums):
        size = edges[flow + 1] - edges[flow]
        gate, up = both[:, :size] * scale, both[:, size : 2 * size] * scale
        hidden += cube_gather((jax.nn.silu(gate) * up).astype(BF16), ORDERS[flow])
    blocks = jnp.stack([block_at(flow) for flow in range(FLOWS)])
    products = down(blocks, hidden, w_down)
    return (state + sum_over_chips(sum_over_cores(*products))).astype(BF16)


def solution(mesh):
    in_specs = (
        P(("attn", "ffn"), None),
        P(("attn", "ffn"), None, None),
        P(("attn", "ffn"), None, None),
        P(("attn", "ffn"), None),
        P(("attn", "ffn"), None),
        P(("attn", "ffn")),
        P(),
        P(None, "attn"),
        P("ffn", "attn"),
        P("attn"),
        P("attn", "ffn"),
        P("attn", "ffn"),
        P("ffn", "attn"),
    )
    out_specs = P("ffn", "attn")
    return jax.shard_map(local, mesh=mesh, in_specs=in_specs, out_specs=out_specs, check_vma=False)
```

```python
import functools

import jax
import jax.numpy as jnp
from jax import lax
from jax.experimental import pallas as pl
from jax.experimental.pallas import tpu as pltpu
from jax.sharding import PartitionSpec as P

QUERY_HEADS = 64
KEY_VALUE_HEADS = 4
HEAD_SIZE = 128
SLOT_CAPACITY = 256

epsilon = 1e-05

F32, BF16 = jnp.float32, jnp.bfloat16
LANES = 128
FLOWS = 3

ATTN, FFN = 8, 16
SAME_CORE = [[2 * chip + core for chip in range(FFN // 2)] for core in range(2)]


def over_core(value):
    pairs = [(n, n ^ 1) for n in range(FFN)]
    return lax.ppermute(value, "ffn", pairs)


def over_chips(blocks):
    return lax.all_to_all(blocks, "ffn", 0, 0, tiled=True, axis_index_groups=SAME_CORE)


AXES = ((2, 4, 1), (4, 1, 2))
ORDERS = ((0, 1, 2), (1, 2, 0), (2, 0, 1))


def gray(place):
    return place ^ ((place & 4) >> 1)


def over_cube(value, axis):
    pairs = []
    for a in range(ATTN):
        for f in range(FFN):
            to_a = gray(gray(a) ^ AXES[f & 1][axis])
            pairs.append((a * FFN + f, to_a * FFN + f))
    return lax.ppermute(value, ("attn", "ffn"), pairs)


def cube_sum(sent, kept, order):
    for axis in order:
        total = kept.astype(F32) + over_cube(sent, axis).astype(F32)
        middle = total.shape[0] // 2
        sent, kept = total[:middle].astype(BF16), total[middle:]
    return total[0]


def cube_gather(own, order):
    own = own[None]
    for axis in order[:0:-1]:
        own = jnp.concatenate([over_cube(own, axis), own])
    return over_cube(own, order[0]), own


VMEM = pl.BlockSpec(memory_space=pltpu.VMEM)
SMEM = pl.BlockSpec(memory_space=pltpu.SMEM)
HBM = pl.BlockSpec(memory_space=pl.ANY)
TILE = 256
VMEM_LIMIT = 24 * 2**20


def load_kernel(count, *refs):
    arrived = refs[-1]
    copies = [
        pltpu.make_async_copy(refs[n], refs[count + n], arrived.at[n]) for n in range(count)
    ]
    for copy in copies:
        copy.start()
    for copy in copies:
        copy.wait()


def load(*arrays):
    count = len(arrays)
    return pl.pallas_call(
        functools.partial(load_kernel, count),
        out_shape=[jax.ShapeDtypeStruct(array.shape, array.dtype) for array in arrays],
        in_specs=[HBM] * count,
        out_specs=[VMEM] * count,
        scratch_shapes=[pltpu.SemaphoreType.DMA((count,))],
        compiler_params=pltpu.CompilerParams(vmem_limit_bytes=VMEM_LIMIT),
        cost_estimate=pl.CostEstimate(
            flops=0,
            bytes_accessed=sum(2 * array.size * array.dtype.itemsize for array in arrays),
            transcendentals=0,
        ),
    )(*arrays)


def gate_up_kernel(cut, place, x, w_gate, w_up, sent, kept, placed):
    batch = sent.shape[1]

    def store(value, at):
        for block in range(ATTN):
            part = value[block * batch : (block + 1) * batch]
            placed[place[block], :, at : at + value.shape[1]] = part

    at = 0
    for weights in (w_gate, w_up):
        for start in range(cut.start, cut.stop, TILE):
            columns = slice(start, min(start + TILE, cut.stop))
            product = jnp.dot(x[...], weights[:, columns], preferred_element_type=F32)
            store(product.astype(BF16), at)
            at += columns.stop - columns.start
    sent[...] = placed[: ATTN // 2]
    kept[...] = placed[ATTN // 2 :]


def first_gate_up_kernel(cut, place, own, other, w_gate, w_up, sent, kept, x, placed):
    depth = x.shape[1]
    half = own.shape[0]
    x[:half] = own[:, :depth]
    x[half:] = other[:, :depth]
    batch = sent.shape[1]
    for block in range(ATTN):
        rows, row = (own, block * batch) if block < ATTN // 2 else (other, block * batch - half)
        placed[place[block], :, 2 * (cut.stop - cut.start) :] = rows[row : row + batch, depth:]
    gate_up_kernel(cut, place, x, w_gate, w_up, sent, kept, placed)


def gate_up(place, x, w_gate, w_up, cut):
    depth = w_gate.shape[0]
    rows = sum(part.shape[0] for part in x)
    width = 2 * (cut.stop - cut.start) + x[0].shape[1] - depth
    half = jax.ShapeDtypeStruct((ATTN // 2, rows // ATTN, width), BF16)
    whole = [jax.ShapeDtypeStruct((rows, depth), BF16)] * (len(x) - 1)
    body = first_gate_up_kernel if whole else gate_up_kernel
    return pl.pallas_call(
        functools.partial(body, cut),
        out_shape=[half, half] + whole,
        in_specs=[SMEM] + [VMEM] * (len(x) + 2),
        out_specs=[VMEM] * (2 + len(whole)),
        scratch_shapes=[pltpu.VMEM((ATTN, rows // ATTN, width), BF16)],
        compiler_params=pltpu.CompilerParams(vmem_limit_bytes=VMEM_LIMIT),
        cost_estimate=pl.CostEstimate(
            flops=2 * rows * depth * width,
            bytes_accessed=2 * depth * width + 2 * rows * depth,
            transcendentals=0,
        ),
    )(place, *x, w_gate, w_up)


def down_kernel(place, *refs):
    parts, (w_down, own, other, hidden) = refs[: 2 * FLOWS], refs[2 * FLOWS :]
    at = 0
    for flow in range(FLOWS):
        batch, width = parts[2 * flow].shape[1:]
        for block in range(ATTN):
            part = parts[2 * flow + block // (ATTN // 2)][block % (ATTN // 2)]
            row = pl.multiple_of(place[flow, block] * batch, batch)
            hidden[pl.ds(row, batch), at : at + width] = part
        at += width
    half = own.shape[0]
    for start in range(0, own.shape[1], TILE):
        columns = slice(start, start + TILE)
        product = jnp.dot(hidden[...], w_down[:, columns], preferred_element_type=F32)
        own[:, columns] = product[:half]
        other[:, columns] = product[half:].astype(BF16)


def down(place, parts, w_down):
    units, width = w_down.shape
    rows = ATTN * parts[0].shape[1]
    return pl.pallas_call(
        down_kernel,
        out_shape=(
            jax.ShapeDtypeStruct((rows // 2, width), F32),
            jax.ShapeDtypeStruct((rows // 2, width), BF16),
        ),
        in_specs=[SMEM] + [VMEM] * (2 * FLOWS) + [VMEM],
        out_specs=(VMEM, VMEM),
        scratch_shapes=[pltpu.VMEM((rows, units), BF16)],
        compiler_params=pltpu.CompilerParams(vmem_limit_bytes=VMEM_LIMIT),
        cost_estimate=pl.CostEstimate(
            flops=2 * rows * units * width,
            bytes_accessed=2 * units * width + 2 * rows * units + 3 * rows * width,
            transcendentals=0,
        ),
    )(place, *parts, w_down)


def copies(value):
    return lax.optimization_barrier(jnp.broadcast_to(value, (8,) + value.shape))


def attend_kernel(lengths, queries, keys, values, own_key, own_value, out, heads, held, arrived, done):
    slots = queries.shape[0]
    group = QUERY_HEADS // KEY_VALUE_HEADS
    features = out.shape[2]
    fetches = []
    for slot in range(slots):
        fetches.append(
            (
                pltpu.make_async_copy(keys.at[slot], held.at[0, slot], arrived.at[0, slot]),
                pltpu.make_async_copy(values.at[slot], held.at[1, slot], arrived.at[1, slot]),
            )
        )
    for pair in fetches:
        for fetch in pair:
            fetch.start()
    wide = queries[...].astype(F32)
    for slot in range(slots):
        for head in range(QUERY_HEADS):
            heads[slot, head : head + 1] = wide[
                slot : slot + 1, head * HEAD_SIZE : (head + 1) * HEAD_SIZE
            ]
    factor = HEAD_SIZE ** (-0.5)
    position = lax.broadcasted_iota(jnp.int32, (QUERY_HEADS, SLOT_CAPACITY), 1)
    for slot in range(slots):
        for fetch in fetches[slot]:
            fetch.wait()
        query = heads[slot]
        own_score, scores = [], []
        for kv in range(KEY_VALUE_HEADS):
            at = slice(kv * HEAD_SIZE, (kv + 1) * HEAD_SIZE)
            part = query[kv * group : (kv + 1) * group]
            scores.append(
                lax.dot_general(
                    part.astype(BF16),
                    held[0, slot, :, at],
                    (((1,), (1,)), ((), ())),
                    preferred_element_type=F32,
                )
            )
            key = own_key[slot : slot + 1, at].astype(F32)
            own_score.append(jnp.sum(part * key, axis=-1, keepdims=True) * factor)
        scores = jnp.where(position < lengths[slot], jnp.concatenate(scores) * factor, -jnp.inf)
        own_score = jnp.concatenate(own_score)
        highest = jnp.maximum(jnp.max(scores, axis=-1, keepdims=True), own_score)
        weights = jnp.exp(scores - highest)
        own_weight = jnp.exp(own_score - highest)
        weight_sum = jnp.sum(weights, axis=-1, keepdims=True) + own_weight
        own_low = own_weight.astype(BF16).astype(F32)
        for kv in range(KEY_VALUE_HEADS):
            at = slice(kv * HEAD_SIZE, (kv + 1) * HEAD_SIZE)
            own_heads = slice(kv * group, (kv + 1) * group)
            combined = jnp.dot(
                weights[own_heads].astype(BF16), held[1, slot, :, at], preferred_element_type=F32
            )
            value = own_value[slot : slot + 1, at].astype(F32)
            combined = (combined + own_low[own_heads] * value) / weight_sum[own_heads]
            for n in range(group):
                first = (kv * group + n) * HEAD_SIZE
                to = first % features
                done[first // features, slot : slot + 1, to : to + HEAD_SIZE] = combined[n : n + 1]
    whole = done[...].astype(BF16)
    for device in range(ATTN):
        out[device * FFN : (device + 1) * FFN] = whole


def attend(queries, slot_key_cache, slot_value_cache, fresh_token_key, fresh_token_value, lengths):
    slots, features = queries.shape[0], QUERY_HEADS * HEAD_SIZE // FFN
    return pl.pallas_call(
        attend_kernel,
        out_shape=jax.ShapeDtypeStruct((ATTN * FFN, slots, features), BF16),
        in_specs=[SMEM, VMEM, HBM, HBM, VMEM, VMEM],
        out_specs=VMEM,
        scratch_shapes=[
            pltpu.VMEM((slots, QUERY_HEADS, HEAD_SIZE), F32),
            pltpu.VMEM((2,) + slot_key_cache.shape, BF16),
            pltpu.SemaphoreType.DMA((2, slots)),
            pltpu.VMEM((FFN, slots, features), F32),
        ],
        compiler_params=pltpu.CompilerParams(vmem_limit_bytes=58 * 2**20),
        cost_estimate=pl.CostEstimate(
            flops=4 * queries.size * SLOT_CAPACITY,
            bytes_accessed=4 * slot_key_cache.size,
            transcendentals=slots * QUERY_HEADS * SLOT_CAPACITY,
        ),
    )(lengths, queries, slot_key_cache, slot_value_cache, fresh_token_key, fresh_token_value)


def local(
    queries,
    slot_key_cache,
    slot_value_cache,
    fresh_token_key,
    fresh_token_value,
    lengths,
    slot_of,
    residual,
    w_out,
    norm_gain,
    w_gate,
    w_up,
    w_down,
):
    f = lax.axis_index("ffn")
    core = f % 2
    slots = queries.shape[0]
    features, width = w_out.shape
    units = w_up.shape[1]
    rows = residual.shape[0]
    share, batch, half = rows // FFN, rows // ATTN, rows // 2
    width_total = width * ATTN

    parts = attend(
        queries, slot_key_cache, slot_value_cache, fresh_token_key, fresh_token_value, lengths
    )
    held = lax.all_to_all(parts, ("attn", "ffn"), 0, 0, tiled=True).reshape(rows, features)

    by_core = slot_of.reshape(FFN // 2, 2, share)
    swapped = jnp.where(core == 0, by_core, by_core[:, ::-1])
    wanted = swapped.transpose(1, 0, 2).reshape(rows)
    choice = (wanted[:, None] == jnp.arange(rows, dtype=jnp.int32)[None, :]).astype(BF16)
    ordered = jnp.dot(choice, held, preferred_element_type=F32).astype(BF16)
    kept = lax.dynamic_slice_in_dim(residual, f * share, share, 0).astype(F32)

    def sum_over_cores(own, other):
        total = own + over_core(other).astype(F32)
        return total.astype(BF16).reshape(FFN // 2, share, width)

    def sum_over_chips(blocks):
        return jnp.sum(over_chips(blocks).astype(F32), axis=0)

    other = jnp.dot(ordered[half:], w_out, preferred_element_type=F32).astype(BF16)
    blocks = sum_over_cores(jnp.dot(ordered[:half], w_out, preferred_element_type=F32), other)
    blocks, w_up = lax.optimization_barrier((blocks, w_up))
    (w_up,) = load(w_up)
    blocks, w_up = lax.optimization_barrier((over_chips(blocks), w_up))
    state = kept + jnp.sum(blocks.astype(F32), axis=0)
    state, w_gate = lax.optimization_barrier((state, w_gate))
    (w_gate,) = load(w_gate)
    squares = jnp.sum(state * state, axis=-1, keepdims=True)
    scaled = jnp.concatenate(
        [state * norm_gain.astype(F32), jnp.broadcast_to(squares, (share, LANES))], axis=1
    )
    scaled = over_chips(copies(scaled.astype(BF16))).reshape(half, width + LANES)
    x = [scaled, over_core(scaled)]

    eight = jnp.arange(ATTN, dtype=jnp.int32)
    attn_at = gray(lax.axis_index("attn"))

    def masks(flow):
        return [jnp.where(core == 0, AXES[0][axis], AXES[1][axis]) for axis in ORDERS[flow]]

    def place_of(flow):
        flipped = attn_at ^ gray(eight)
        bits = [((flipped & mask) == 0).astype(jnp.int32) for mask in masks(flow)]
        return bits[0] * 4 + bits[1] * 2 + bits[2]

    def block_at(flow):
        flips = [(1 - ((eight >> (2 - n)) & 1)) * mask for n, mask in enumerate(masks(flow))]
        return gray(attn_at ^ flips[0] ^ flips[1] ^ flips[2])

    tiles = units // LANES
    edges = [tiles * flow // FLOWS * LANES for flow in range(FLOWS + 1)]
    sums = []
    for flow in range(FLOWS):
        sent, kept, *whole = gate_up(
            place_of(flow), x, w_gate, w_up, slice(edges[flow], edges[flow + 1])
        )
        x = whole or x
        sums.append(cube_sum(sent, kept, ORDERS[flow]))
    sums[0], w_down = lax.optimization_barrier((sums[0], w_down))
    (w_down,) = load(w_down)
    scale = lax.rsqrt(sums[0][:, -1:] / width_total + epsilon)
    hidden = []
    for flow, both in enumerate(sums):
        size = edges[flow + 1] - edges[flow]
        gate, up = both[:, :size] * scale, both[:, size : 2 * size] * scale
        hidden += cube_gather((jax.nn.silu(gate) * up).astype(BF16), ORDERS[flow])
    blocks = jnp.stack([block_at(flow) for flow in range(FLOWS)])
    products = down(blocks, hidden, w_down)
    return (state + sum_over_chips(sum_over_cores(*products))).astype(BF16)


def solution(mesh):
    in_specs = (
        P(("attn", "ffn"), None),
        P(("attn", "ffn"), None, None),
        P(("attn", "ffn"), None, None),
        P(("attn", "ffn"), None),
        P(("attn", "ffn"), None),
        P(("attn", "ffn")),
        P(),
        P(None, "attn"),
        P("ffn", "attn"),
        P("attn"),
        P("attn", "ffn"),
        P("attn", "ffn"),
        P("ffn", "attn"),
    )
    out_specs = P("ffn", "attn")
    return jax.shard_map(local, mesh=mesh, in_specs=in_specs, out_specs=out_specs, check_vma=False)
```
